32 devices in a mesh: gx: 4 (over z), gy: 4 (over y, x), gz: 2 (over core).
Axes of the slice: x: 2, y: 2, z: 4, core: 2. Of those that a mesh axis runs over, the one named last changes fastest.
Arguments:
- f_pop: float32 [19, 16, 64, 256], P(None, 'gx', 'gy', 'gz'), may hold values from 0.02 to 0.1
- g_pop: float32 [19, 16, 64, 256], P(None, 'gx', 'gy', 'gz'), may hold values from -0.2 to 0.2
- displacement: int32 [1], replicated, may hold values from 33 to 47
Outputs:
- f_new: float32 [19, 16, 64, 256], P(None, 'gx', 'gy', 'gz')
- g_new: float32 [19, 16, 64, 256], P(None, 'gx', 'gy', 'gz')
The draws below stay inside these ranges and needn't reach their ends.
All inputs are finite; a program needn't handle non-finite values.
Results may differ from the reference program's by a relative error of at most 0.0001.
Values sent between devices are 32-bit elements; how exact they have to be, the bound alone decides.
A program may use at most 64 MiB of HBM per device.

```python
import jax
import jax.numpy as jnp

CX = 4
CY = 16
POPS = 19
NX = 16
NY = 64
NZ = 256


def steps_of(stream_key, dims, pieces, low, top_value):
    loudness, own = 1.0, jax.random.fold_in(stream_key, 6)
    for position, parts in pieces:
        draws = jnp.exp(jax.random.uniform(jax.random.fold_in(own, position), (parts,), jnp.float32, low / len(pieces), top_value / len(pieces)))
        loudness = loudness * jnp.repeat(draws, dims[position] // parts).reshape([-1 if axis == position else 1 for axis in range(len(dims))])
    return loudness


def setup_inputs(seed: int = 0) -> dict:
    key_list = jax.random.split(jax.random.key(seed), 4)
    return {
        "f_pop": jnp.clip(0.02 + 0.08 * jax.random.uniform(key_list[0], (POPS, NX, NY, NZ), jnp.float32) ** steps_of(key_list[0], (POPS, NX, NY, NZ), ((1, 4), (2, 4), (3, 2)), -0.2, 0.2), 0.02, 0.1),
        "g_pop": jnp.clip(jax.random.uniform(key_list[1], (POPS, NX, NY, NZ), jnp.float32, -0.2, 0.2) * steps_of(key_list[1], (POPS, NX, NY, NZ), ((1, 4), (2, 4), (3, 2)), -0.4, 0.0), -0.2, 0.2),
        "displacement": jax.random.randint(key_list[2], (1,), NY // 2 + 1, NY // 2 + CY).astype(jnp.int32),
    }


VELOCITIES = [(0, 0, 0), (1, 0, 0), (1, 1, 0), (1, -1, 0), (1, 0, 1), (1, 0, -1),
              (-1, 0, 0), (-1, -1, 0), (-1, 1, 0), (-1, 0, -1), (-1, 0, 1),
              (0, 1, 0), (0, -1, 0), (0, 0, 1), (0, 0, -1), (0, 1, 1), (0, -1, -1), (0, 1, -1), (0, -1, 1)]
BULK_COEF = 0.5
STIFFNESS = 0.5
TAU_FLUID = 0.8
TAU_ORDER = 0.9


def lattice_weight(number):
    steps_sq = sum(abs(comp) for comp in VELOCITIES[number])
    if steps_sq == 0:
        return 1.0 / 3.0
    if steps_sq == 1:
        return 1.0 / 18.0
    return 1.0 / 36.0


def along(number, values, base):
    result = jnp.zeros_like(base)
    for axis_id in range(3):
        comp = VELOCITIES[number][axis_id]
        if comp != 0:
            result = result + comp * values[axis_id]
    return result


def collide(f_pop, g_pop, order_field, laplace, slopes):
    density = jnp.sum(f_pop, axis=0)
    chemical = BULK_COEF * (order_field * order_field * order_field - order_field) - STIFFNESS * laplace
    forces = [chemical * slope for slope in slopes]
    moments = []
    for axis_id in range(3):
        moment = jnp.zeros_like(density)
        for number in range(19):
            comp = VELOCITIES[number][axis_id]
            if comp != 0:
                moment = moment + comp * f_pop[number]
        moments.append(moment)
    flows = [(moments[axis_id] + 0.5 * forces[axis_id]) / density for axis_id in range(3)]
    speed_sq = flows[0] * flows[0] + flows[1] * flows[1] + flows[2] * flows[2]
    flow_force = flows[0] * forces[0] + flows[1] * forces[1] + flows[2] * forces[2]
    f_posts = []
    g_eqs = []
    for number in range(19):
        weight = lattice_weight(number)
        proj_flow = along(number, flows, density)
        proj_force = along(number, forces, density)
        shape_term = 3.0 * proj_flow + 4.5 * proj_flow * proj_flow - 1.5 * speed_sq
        f_eq = weight * density * (1.0 + shape_term)
        source = (1.0 - 0.5 / TAU_FLUID) * weight * (3.0 * (proj_force - flow_force) + 9.0 * proj_flow * proj_force)
        f_posts.append(f_pop[number] - (f_pop[number] - f_eq) / TAU_FLUID + source)
        g_eqs.append(weight * (3.0 * chemical + order_field * shape_term))
    rest_eq = order_field
    for number in range(1, 19):
        rest_eq = rest_eq - g_eqs[number]
    g_eqs[0] = rest_eq
    g_posts = [g_pop[number] - (g_pop[number] - g_eqs[number]) / TAU_ORDER for number in range(19)]
    return f_posts, g_posts


def stream(posts, shift, at_low, at_high):
    results = []
    for number in range(19):
        vel_x, vel_y, vel_z = VELOCITIES[number]
        plain = jnp.roll(posts[number], (vel_x, vel_y, vel_z), (0, 1, 2))
        if vel_x == 1:
            plain = jnp.where(at_low, jnp.roll(plain, shift, 1), plain)
        if vel_x == -1:
            plain = jnp.where(at_high, jnp.roll(plain, -shift, 1), plain)
        results.append(plain)
    return jnp.stack(results)


def reference(f_pop, g_pop, displacement):
    shift = displacement[0]
    order_field = jnp.sum(g_pop, axis=0)
    plane = jnp.arange(order_field.shape[0]) % CX
    at_low = (plane == 0)[:, None, None]
    at_high = (plane == CX - 1)[:, None, None]
    back_x = jnp.roll(order_field, 1, 0)
    neigh_xm = jnp.where(at_low, jnp.roll(back_x, shift, 1), back_x)
    fore_x = jnp.roll(order_field, -1, 0)
    neigh_xp = jnp.where(at_high, jnp.roll(fore_x, -shift, 1), fore_x)
    neigh_ym = jnp.roll(order_field, 1, 1)
    neigh_yp = jnp.roll(order_field, -1, 1)
    neigh_zm = jnp.roll(order_field, 1, 2)
    neigh_zp = jnp.roll(order_field, -1, 2)
    laplace = neigh_xm + neigh_xp + neigh_ym + neigh_yp + neigh_zm + neigh_zp - 6.0 * order_field
    slopes = [0.5 * (neigh_xp - neigh_xm), 0.5 * (neigh_yp - neigh_ym), 0.5 * (neigh_zp - neigh_zm)]
    f_posts, g_posts = collide(f_pop, g_pop, order_field, laplace, slopes)
    f_new = stream(f_posts, shift, at_low, at_high)
    g_new = stream(g_posts, shift, at_low, at_high)
    return f_new, g_new
```

```python
import functools

import jax
import jax.numpy as jnp
from jax import lax
from jax.experimental import pallas as pl
from jax.experimental.pallas import tpu as pltpu
from jax.sharding import PartitionSpec as P

VELOCITIES = [
    (0, 0, 0),
    (1, 0, 0),
    (1, 1, 0),
    (1, -1, 0),
    (1, 0, 1),
    (1, 0, -1),
    (-1, 0, 0),
    (-1, -1, 0),
    (-1, 1, 0),
    (-1, 0, -1),
    (-1, 0, 1),
    (0, 1, 0),
    (0, -1, 0),
    (0, 0, 1),
    (0, 0, -1),
    (0, 1, 1),
    (0, -1, -1),
    (0, 1, -1),
    (0, -1, 1),
]
POPS = 19
TAU_FLUID = 0.8
TAU_ORDER = 0.9
PAIRS = [(1, 6), (2, 7), (3, 8), (4, 9), (5, 10), (11, 12), (13, 14), (15, 16), (17, 18)]
Z_PAIRS = [(4, 5), (10, 9), (13, 14), (15, 16), (18, 17)]
Y_UP = [2, 8, 11, 15, 17]
Y_DOWN = [3, 7, 12, 16, 18]
UP = [(0, 1), (0, 2), (0, 3), (1, 1), (1, 2), (1, 3), (0, 4), (0, 5), (1, 4), (1, 5)]
DOWN = [(0, 6), (0, 7), (0, 8), (1, 6), (1, 7), (1, 8), (0, 9), (0, 10), (1, 9), (1, 10)]
FIRST = 6
MESH = pl.DeviceIdType.MESH


def kernel(
    sizes,
    shift_ref,
    f_hbm,
    g_hbm,
    f_out,
    g_out,
    f_ref,
    g_ref,
    phi_ref,
    phi_z,
    phi_ys,
    phi_yr,
    phi_lo,
    phi_hi,
    q_ref,
    z_send,
    z_recv,
    up_send,
    down_send,
    lo_one,
    lo_two,
    hi_one,
    hi_two,
    y_send,
    y_recv,
    local_sem,
    send_sem,
    recv_sem,
):
    count_x, count_y, count_z = sizes
    planes, rows, lanes = f_ref.shape[1:]
    a, b, c = lax.axis_index("gx"), lax.axis_index("gy"), lax.axis_index("gz")
    half = count_y // 2

    def at(dx, dy, dz=0):
        return (
            lax.rem(a + dx + count_x, count_x),
            lax.rem(b + dy + count_y, count_y),
            lax.rem(c + dz, count_z),
        )

    next_near, next_far = at(1, half), at(1, half + 1)
    prev_near, prev_far = at(-1, -half), at(-1, -half - 1)
    y_next, y_prev, z_other = at(0, 1), at(0, -1), at(0, 0, 1)

    load_g = pltpu.make_async_copy(g_hbm, g_ref, local_sem.at[0])
    load_f = pltpu.make_async_copy(f_hbm, f_ref, local_sem.at[1])
    load_g.start()
    load_f.start()
    barrier = pltpu.get_barrier_semaphore()
    partners = (next_near, next_far, prev_near, prev_far, y_next, y_prev, z_other)
    for partner in partners:
        pl.semaphore_signal(barrier, inc=1, device_id=partner, device_id_type=MESH)

    used = [0]

    def send(src, dst, target):
        slot = used[0]
        used[0] += 1
        copy = pltpu.make_async_remote_copy(
            src_ref=src,
            dst_ref=dst,
            send_sem=send_sem.at[slot],
            recv_sem=recv_sem.at[slot],
            device_id=target,
            device_id_type=MESH,
        )
        copy.start()
        return copy

    load_g.wait()
    for x in range(planes):
        parts = [g_ref[i, x] for i in range(POPS)]
        while len(parts) > 1:
            parts = [
                parts[k] + parts[k + 1] if k + 1 < len(parts) else parts[k]
                for k in range(0, len(parts), 2)
            ]
        phi_ref[x + 1] = parts[0]
        phi_ys[0, x : x + 1, :] = parts[0][rows - 1 : rows]
        phi_ys[1, x : x + 1, :] = parts[0][0:1]
    pl.semaphore_wait(barrier, len(partners))

    low, high = pl.ds(0, rows), pl.ds(rows, rows)
    last = planes
    slides = [
        send(phi_ref.at[last], phi_lo.at[low], next_far),
        send(phi_ref.at[last], phi_lo.at[high], next_near),
        send(phi_ref.at[1], phi_hi.at[low], prev_near),
        send(phi_ref.at[1], phi_hi.at[high], prev_far),
    ]
    to_z = send(phi_ref.at[pl.ds(1, planes)], phi_z, z_other)
    to_up = send(phi_ys.at[0], phi_yr.at[0], y_next)
    to_down = send(phi_ys.at[1], phi_yr.at[1], y_prev)

    lane = lax.broadcasted_iota(jnp.int32, (rows, lanes), 1)
    row = lax.broadcasted_iota(jnp.int32, (rows, lanes), 0)
    lane_first, lane_last = lane == 0, lane == lanes - 1
    row_first, row_last = row == 0, row == rows - 1
    residue = jnp.clip(shift_ref[0] - half * rows, 1, rows - 1)

    def collide(x, put):
        phi = phi_ref[x + 1]
        xm, xp = phi_ref[x], phi_ref[x + 2]
        ym = jnp.where(row_first, phi_yr[0, pl.ds(x, 1), :], pltpu.roll(phi, 1, 0))
        yp = jnp.where(row_last, phi_yr[1, pl.ds(x, 1), :], pltpu.roll(phi, rows - 1, 0))
        other = phi_z[x]
        zm = pltpu.roll(jnp.where(lane_last, other, phi), 1, 1)
        zp = pltpu.roll(jnp.where(lane_first, other, phi), lanes - 1, 1)
        laplace = xm + xp + ym + yp + zm + zp - 6.0 * phi
        chemical = 0.5 * (phi * phi * phi - phi) - 0.5 * laplace
        half_mu = 0.5 * chemical
        force = [half_mu * (xp - xm), half_mu * (yp - ym), half_mu * (zp - zm)]
        f = [f_ref[i, x] for i in range(POPS)]
        even_sum = f[0]
        moment = [None, None, None]
        for plus, minus in PAIRS:
            even_sum = even_sum + (f[plus] + f[minus])
            diff = f[plus] - f[minus]
            for axis in range(3):
                comp = VELOCITIES[plus][axis]
                if comp:
                    if moment[axis] is None:
                        moment[axis] = diff
                    elif comp > 0:
                        moment[axis] = moment[axis] + diff
                    else:
                        moment[axis] = moment[axis] - diff
        density = even_sum
        inverse = 1.0 / density
        flow = [(moment[axis] + 0.5 * force[axis]) * inverse for axis in range(3)]
        usq = flow[0] * flow[0] + flow[1] * flow[1] + flow[2] * flow[2]
        flow_force = flow[0] * force[0] + flow[1] * force[1] + flow[2] * force[2]

        inv_f, inv_g = 1.0 / TAU_FLUID, 1.0 / TAU_ORDER
        keep_f, keep_g = 1.0 - inv_f, 1.0 - inv_g
        gain = 1.0 - 0.5 / TAU_FLUID
        f_base = inv_f * density * (1.0 - 1.5 * usq) - (3.0 * gain) * flow_force
        f_square = (4.5 * inv_f) * density
        f_line = (3.0 * inv_f) * density
        g_base = inv_g * (3.0 * chemical - 1.5 * phi * usq)
        g_square = (4.5 * inv_g) * phi
        g_line = (3.0 * inv_g) * phi
        put(0, 0, keep_f * f[0] + (1.0 / 3.0) * f_base)
        put(1, 0, keep_g * g_ref[0, x] + inv_g * (phi - 2.0 * chemical - 0.5 * phi * usq))

        def dot(number, values):
            total = None
            for axis in range(3):
                comp = VELOCITIES[number][axis]
                if comp:
                    if total is None:
                        total = values[axis] if comp > 0 else -values[axis]
                    else:
                        total = total + values[axis] if comp > 0 else total - values[axis]
            return total

        done = {}
        for plus, minus in PAIRS:
            weight = 1.0 / 18.0 if sum(abs(v) for v in VELOCITIES[plus]) == 1 else 1.0 / 36.0
            cu = dot(plus, flow)
            cf = dot(plus, force)
            f_even = weight * (f_base + cu * (f_square * cu + (9.0 * gain) * cf))
            f_odd = weight * (f_line * cu + (3.0 * gain) * cf)
            g_even = weight * (g_base + g_square * (cu * cu))
            g_odd = weight * (g_line * cu)
            done[0, plus] = keep_f * f[plus] + (f_even + f_odd)
            done[0, minus] = keep_f * f[minus] + (f_even - f_odd)
            done[1, plus] = keep_g * g_ref[plus, x] + (g_even + g_odd)
            done[1, minus] = keep_g * g_ref[minus, x] + (g_even - g_odd)
        for (field, number), value in done.items():
            put(field, number, value)
        for field in range(2):
            for k, (plus, minus) in enumerate(Z_PAIRS):
                z_send[x, field * 5 + k] = jnp.where(
                    lane_last, done[field, plus], done[field, minus]
                )

    to_z.wait_recv()
    to_up.wait_recv()
    to_down.wait_recv()
    load_f.wait()

    def inner(x, carry):
        def put(field, number, value):
            q_ref[field * POPS + number, x + VELOCITIES[number][0]] = value

        collide(x, put)
        return carry

    lax.fori_loop(1, planes - 1, inner, 0)
    middle = pl.ds(1, planes - 2)
    z_mid = send(z_send.at[middle], z_recv.at[middle], z_other)

    def put_top(field, number, value):
        if VELOCITIES[number][0] == 1:
            up_send[UP.index((field, number))] = value
        else:
            q_ref[field * POPS + number, planes - 1 + VELOCITIES[number][0]] = value

    def put_bottom(field, number, value):
        if VELOCITIES[number][0] == -1:
            down_send[DOWN.index((field, number))] = value
        else:
            q_ref[field * POPS + number, VELOCITIES[number][0]] = value

    for copy in slides:
        copy.wait()
    start_lo, start_hi = rows - residue, residue
    phi_ref[0] = phi_lo[pl.ds(start_lo, rows), :]
    phi_ref[planes + 1] = phi_hi[pl.ds(start_hi, rows), :]

    part_one, part_two = pl.ds(0, FIRST), pl.ds(FIRST, len(UP) - FIRST)

    def send_up(part, recv):
        return [
            send(up_send.at[part], recv.at[:, high], next_near),
            send(up_send.at[part], recv.at[:, low], next_far),
        ]

    def send_down(part, recv):
        return [
            send(down_send.at[part], recv.at[:, low], prev_near),
            send(down_send.at[part], recv.at[:, high], prev_far),
        ]

    collide(planes - 1, put_top)
    first_up = send_up(part_one, lo_one)
    z_top = send(z_send.at[planes - 1], z_recv.at[planes - 1], z_other)
    collide(0, put_bottom)
    first_down = send_down(part_one, hi_one)
    z_bottom = send(z_send.at[0], z_recv.at[0], z_other)

    def along_z(x, k, field, number, value):
        plane = z_recv[x, field * 5 + k]
        if VELOCITIES[number][2] == 1:
            return pltpu.roll(jnp.where(lane_last, plane, value), 1, 1)
        return pltpu.roll(jnp.where(lane_first, plane, value), lanes - 1, 1)

    z_top.wait_recv()
    for field in range(2):
        for number in (4, 5):
            slot = UP.index((field, number))
            up_send[slot] = along_z(planes - 1, 0, field, number, up_send[slot])
    second_up = send_up(part_two, lo_two)
    z_bottom.wait_recv()
    for field in range(2):
        for number in (9, 10):
            slot = DOWN.index((field, number))
            down_send[slot] = along_z(0, 1, field, number, down_send[slot])
    second_down = send_down(part_two, hi_two)
    z_mid.wait_recv()

    for field in range(2):
        for k, pair in enumerate(Z_PAIRS):
            for number in pair:
                step = VELOCITIES[number][0]
                for x in range(max(0, -step), planes - max(0, step)):
                    index = field * POPS + number
                    q_ref[index, x + step] = along_z(x, k, field, number, q_ref[index, x + step])

    def stays(number):
        step = VELOCITIES[number][0]
        return range(max(0, step), planes + min(0, step))

    for field in range(2):
        for k in range(5):
            for side, numbers, edge in ((0, Y_UP, rows - 1), (1, Y_DOWN, 0)):
                for x in stays(numbers[k]):
                    spot = (field * 5 + k) * planes + x
                    y_send[side, spot : spot + 1, :] = q_ref[
                        field * POPS + numbers[k], x, edge : edge + 1, :
                    ]
    y_up = send(y_send.at[0], y_recv.at[0], y_next)
    y_down = send(y_send.at[1], y_recv.at[1], y_prev)
    y_up.wait_recv()
    y_down.wait_recv()
    for field in range(2):
        for k in range(5):
            for x in stays(Y_UP[k]):
                spot = (field * 5 + k) * planes + x
                index = field * POPS + Y_UP[k]
                q_ref[index, x] = jnp.where(
                    row_first, y_recv[0, spot : spot + 1, :], pltpu.roll(q_ref[index, x], 1, 0)
                )
            for x in stays(Y_DOWN[k]):
                spot = (field * 5 + k) * planes + x
                index = field * POPS + Y_DOWN[k]
                q_ref[index, x] = jnp.where(
                    row_last,
                    y_recv[1, spot : spot + 1, :],
                    pltpu.roll(q_ref[index, x], rows - 1, 0),
                )

    stores = []

    def store(field, pops, span):
        out = (f_out, g_out)[field]
        lo, hi = pops
        copy = pltpu.make_async_copy(
            q_ref.at[pl.ds(field * POPS + lo, hi - lo), span],
            out.at[pl.ds(lo, hi - lo), span],
            local_sem.at[2 + len(stores)],
        )
        copy.start()
        stores.append(copy)

    for field in range(2):
        store(field, (0, 1), pl.ds(0, planes))
        store(field, (1, 6), pl.ds(1, planes - 1))
        store(field, (6, 11), pl.ds(0, planes - 1))
        store(field, (11, POPS), pl.ds(0, planes))

    def land(offset, lo_recv, hi_recv):
        for slot in range(lo_recv.shape[0]):
            field, number = UP[offset + slot]
            begin = start_lo - VELOCITIES[number][1]
            q_ref[field * POPS + number, 0] = lo_recv[slot, pl.ds(begin, rows), :]
            field, number = DOWN[offset + slot]
            begin = start_hi - VELOCITIES[number][1]
            q_ref[field * POPS + number, planes - 1] = hi_recv[slot, pl.ds(begin, rows), :]

    for copy in first_up + first_down:
        copy.wait()
    land(0, lo_one, hi_one)
    for copy in second_up + second_down:
        copy.wait()
    land(FIRST, lo_two, hi_two)
    for field in range(2):
        store(field, (1, 6), pl.ds(0, 1))
        store(field, (6, 11), pl.ds(planes - 1, 1))
    for copy in (to_z, to_up, to_down, z_mid, z_top, z_bottom, y_up, y_down):
        copy.wait_send()
    for copy in stores:
        copy.wait()


def local(sizes, f_pop, g_pop, displacement):
    planes, rows, lanes = f_pop.shape[1:]
    block = (rows, lanes)
    f32 = jnp.float32
    crossing = len(UP)
    copies = 20
    return pl.pallas_call(
        functools.partial(kernel, sizes),
        out_shape=(
            jax.ShapeDtypeStruct(f_pop.shape, f32),
            jax.ShapeDtypeStruct(g_pop.shape, f32),
        ),
        in_specs=[
            pl.BlockSpec(memory_space=pltpu.SMEM),
            pl.BlockSpec(memory_space=pl.ANY),
            pl.BlockSpec(memory_space=pl.ANY),
        ],
        out_specs=[pl.BlockSpec(memory_space=pl.ANY)] * 2,
        scratch_shapes=[
            pltpu.VMEM(f_pop.shape, f32),
            pltpu.VMEM(g_pop.shape, f32),
            pltpu.VMEM((planes + 2,) + block, f32),
            pltpu.VMEM((planes,) + block, f32),
            pltpu.VMEM((2, planes, lanes), f32),
            pltpu.VMEM((2, planes, lanes), f32),
            pltpu.VMEM((2 * rows, lanes), f32),
            pltpu.VMEM((2 * rows, lanes), f32),
            pltpu.VMEM((2 * POPS, planes) + block, f32),
            pltpu.VMEM((planes, 10) + block, f32),
            pltpu.VMEM((planes, 10) + block, f32),
            pltpu.VMEM((crossing,) + block, f32),
            pltpu.VMEM((crossing,) + block, f32),
            pltpu.VMEM((FIRST, 2 * rows, lanes), f32),
            pltpu.VMEM((crossing - FIRST, 2 * rows, lanes), f32),
            pltpu.VMEM((FIRST, 2 * rows, lanes), f32),
            pltpu.VMEM((crossing - FIRST, 2 * rows, lanes), f32),
            pltpu.VMEM((2, 10 * planes, lanes), f32),
            pltpu.VMEM((2, 10 * planes, lanes), f32),
            pltpu.SemaphoreType.DMA((14,)),
            pltpu.SemaphoreType.DMA((copies,)),
            pltpu.SemaphoreType.DMA((copies,)),
        ],
        compiler_params=pltpu.CompilerParams(
            collective_id=0, has_side_effects=True, vmem_limit_bytes=24 * 1024 * 1024
        ),
    )(displacement, f_pop, g_pop)


def solution(mesh):
    sizes = tuple(mesh.shape[axis] for axis in ("gx", "gy", "gz"))
    return jax.shard_map(
        functools.partial(local, sizes),
        mesh=mesh,
        in_specs=(P(None, "gx", "gy", "gz"), P(None, "gx", "gy", "gz"), P()),
        out_specs=(P(None, "gx", "gy", "gz"), P(None, "gx", "gy", "gz")),
        check_vma=False,
    )
```

```python
import functools

import jax
import jax.numpy as jnp
from jax import lax
from jax.experimental import pallas as pl
from jax.experimental.pallas import tpu as pltpu
from jax.sharding import PartitionSpec as P

VELOCITIES = [
    (0, 0, 0),
    (1, 0, 0),
    (1, 1, 0),
    (1, -1, 0),
    (1, 0, 1),
    (1, 0, -1),
    (-1, 0, 0),
    (-1, -1, 0),
    (-1, 1, 0),
    (-1, 0, -1),
    (-1, 0, 1),
    (0, 1, 0),
    (0, -1, 0),
    (0, 0, 1),
    (0, 0, -1),
    (0, 1, 1),
    (0, -1, -1),
    (0, 1, -1),
    (0, -1, 1),
]
POPS = 19
TAU_FLUID = 0.8
TAU_ORDER = 0.9
PAIRS = [(1, 6), (2, 7), (3, 8), (4, 9), (5, 10), (11, 12), (13, 14), (15, 16), (17, 18)]
Z_PAIRS = [(4, 5), (10, 9), (13, 14), (15, 16), (18, 17)]
Y_UP = [2, 8, 11, 15, 17]
Y_DOWN = [3, 7, 12, 16, 18]
UP = [(0, 1), (0, 2), (0, 3), (1, 1), (1, 2), (1, 3), (0, 4), (0, 5), (1, 4), (1, 5)]
DOWN = [(0, 6), (0, 7), (0, 8), (1, 6), (1, 7), (1, 8), (0, 9), (0, 10), (1, 9), (1, 10)]
FIRST = 6
MESH = pl.DeviceIdType.MESH


def kernel(
    sizes,
    shift_ref,
    f_hbm,
    g_hbm,
    f_out,
    g_out,
    f_ref,
    g_ref,
    phi_ref,
    phi_z,
    phi_ys,
    phi_yr,
    phi_lo,
    phi_hi,
    z_send,
    z_recv,
    up_send,
    down_send,
    lo_one,
    lo_two,
    hi_one,
    hi_two,
    y_send,
    y_recv,
    local_sem,
    send_sem,
    recv_sem,
):
    count_x, count_y, count_z = sizes
    planes, rows, lanes = f_ref.shape[1:]
    a, b, c = lax.axis_index("gx"), lax.axis_index("gy"), lax.axis_index("gz")
    half = count_y // 2
    outs = (f_out, g_out)

    def at(dx, dy, dz=0):
        return (
            lax.rem(a + dx + count_x, count_x),
            lax.rem(b + dy + count_y, count_y),
            lax.rem(c + dz, count_z),
        )

    next_near, next_far = at(1, half), at(1, half + 1)
    prev_near, prev_far = at(-1, -half), at(-1, -half - 1)
    y_next, y_prev, z_other = at(0, 1), at(0, -1), at(0, 0, 1)

    load_g = pltpu.make_async_copy(g_hbm, g_ref, local_sem.at[0])
    load_f = pltpu.make_async_copy(f_hbm, f_ref, local_sem.at[1])
    load_g.start()
    load_f.start()
    barrier = pltpu.get_barrier_semaphore()
    partners = (next_near, next_far, prev_near, prev_far, y_next, y_prev, z_other)
    for partner in partners:
        pl.semaphore_signal(barrier, inc=1, device_id=partner, device_id_type=MESH)

    used = [0]

    def send(src, dst, target):
        slot = used[0]
        used[0] += 1
        copy = pltpu.make_async_remote_copy(
            src_ref=src,
            dst_ref=dst,
            send_sem=send_sem.at[slot],
            recv_sem=recv_sem.at[slot],
            device_id=target,
            device_id_type=MESH,
        )
        copy.start()
        return copy

    load_g.wait()
    for x in range(planes):
        parts = [g_ref[i, x] for i in range(POPS)]
        while len(parts) > 1:
            parts = [
                parts[k] + parts[k + 1] if k + 1 < len(parts) else parts[k]
                for k in range(0, len(parts), 2)
            ]
        phi_ref[x + 1] = parts[0]
        phi_ys[0, x : x + 1, :] = parts[0][rows - 1 : rows]
        phi_ys[1, x : x + 1, :] = parts[0][0:1]
    pl.semaphore_wait(barrier, len(partners))

    low, high = pl.ds(0, rows), pl.ds(rows, rows)
    last = planes
    slides = [
        send(phi_ref.at[last], phi_lo.at[low], next_far),
        send(phi_ref.at[last], phi_lo.at[high], next_near),
        send(phi_ref.at[1], phi_hi.at[low], prev_near),
        send(phi_ref.at[1], phi_hi.at[high], prev_far),
    ]
    to_z = send(phi_ref.at[pl.ds(1, planes)], phi_z, z_other)
    to_up = send(phi_ys.at[0], phi_yr.at[0], y_next)
    to_down = send(phi_ys.at[1], phi_yr.at[1], y_prev)

    lane = lax.broadcasted_iota(jnp.int32, (rows, lanes), 1)
    row = lax.broadcasted_iota(jnp.int32, (rows, lanes), 0)
    lane_first, lane_last = lane == 0, lane == lanes - 1
    row_first, row_last = row == 0, row == rows - 1
    residue = jnp.clip(shift_ref[0] - half * rows, 1, rows - 1)

    def collide(x, put):
        phi = phi_ref[x + 1]
        xm, xp = phi_ref[x], phi_ref[x + 2]
        ym = jnp.where(row_first, phi_yr[0, pl.ds(x, 1), :], pltpu.roll(phi, 1, 0))
        yp = jnp.where(row_last, phi_yr[1, pl.ds(x, 1), :], pltpu.roll(phi, rows - 1, 0))
        other = phi_z[x]
        zm = pltpu.roll(jnp.where(lane_last, other, phi), 1, 1)
        zp = pltpu.roll(jnp.where(lane_first, other, phi), lanes - 1, 1)
        laplace = xm + xp + ym + yp + zm + zp - 6.0 * phi
        chemical = 0.5 * (phi * phi * phi - phi) - 0.5 * laplace
        half_mu = 0.5 * chemical
        force = [half_mu * (xp - xm), half_mu * (yp - ym), half_mu * (zp - zm)]
        f = [f_ref[i, x] for i in range(POPS)]
        even_sum = f[0]
        moment = [None, None, None]
        for plus, minus in PAIRS:
            even_sum = even_sum + (f[plus] + f[minus])
            diff = f[plus] - f[minus]
            for axis in range(3):
                comp = VELOCITIES[plus][axis]
                if comp:
                    if moment[axis] is None:
                        moment[axis] = diff
                    elif comp > 0:
                        moment[axis] = moment[axis] + diff
                    else:
                        moment[axis] = moment[axis] - diff
        density = even_sum
        inverse = 1.0 / density
        flow = [(moment[axis] + 0.5 * force[axis]) * inverse for axis in range(3)]
        usq = flow[0] * flow[0] + flow[1] * flow[1] + flow[2] * flow[2]
        flow_force = flow[0] * force[0] + flow[1] * force[1] + flow[2] * force[2]

        inv_f, inv_g = 1.0 / TAU_FLUID, 1.0 / TAU_ORDER
        keep_f, keep_g = 1.0 - inv_f, 1.0 - inv_g
        gain = 1.0 - 0.5 / TAU_FLUID
        f_base = inv_f * density * (1.0 - 1.5 * usq) - (3.0 * gain) * flow_force
        f_square = (4.5 * inv_f) * density
        f_line = (3.0 * inv_f) * density
        g_base = inv_g * (3.0 * chemical - 1.5 * phi * usq)
        g_square = (4.5 * inv_g) * phi
        g_line = (3.0 * inv_g) * phi
        put(0, 0, keep_f * f[0] + (1.0 / 3.0) * f_base)
        put(1, 0, keep_g * g_ref[0, x] + inv_g * (phi - 2.0 * chemical - 0.5 * phi * usq))

        def dot(number, values):
            total = None
            for axis in range(3):
                comp = VELOCITIES[number][axis]
                if comp:
                    if total is None:
                        total = values[axis] if comp > 0 else -values[axis]
                    else:
                        total = total + values[axis] if comp > 0 else total - values[axis]
            return total

        done = {}
        for plus, minus in PAIRS:
            weight = 1.0 / 18.0 if sum(abs(v) for v in VELOCITIES[plus]) == 1 else 1.0 / 36.0
            cu = dot(plus, flow)
            cf = dot(plus, force)
            f_even = weight * (f_base + cu * (f_square * cu + (9.0 * gain) * cf))
            f_odd = weight * (f_line * cu + (3.0 * gain) * cf)
            g_even = weight * (g_base + g_square * (cu * cu))
            g_odd = weight * (g_line * cu)
            done[0, plus] = keep_f * f[plus] + (f_even + f_odd)
            done[0, minus] = keep_f * f[minus] + (f_even - f_odd)
            done[1, plus] = keep_g * g_ref[plus, x] + (g_even + g_odd)
            done[1, minus] = keep_g * g_ref[minus, x] + (g_even - g_odd)
        for (field, number), value in done.items():
            put(field, number, value)
        for field in range(2):
            for k, (plus, minus) in enumerate(Z_PAIRS):
                z_send[x, field * 5 + k] = jnp.where(
                    lane_last, done[field, plus], done[field, minus]
                )

    to_z.wait_recv()
    to_up.wait_recv()
    to_down.wait_recv()
    load_f.wait()

    def inner(x, carry):
        def put(field, number, value):
            outs[field][number, x + VELOCITIES[number][0]] = value

        collide(x, put)
        return carry

    lax.fori_loop(1, planes - 1, inner, 0)
    middle = pl.ds(1, planes - 2)
    z_mid = send(z_send.at[middle], z_recv.at[middle], z_other)

    def put_top(field, number, value):
        if VELOCITIES[number][0] == 1:
            up_send[UP.index((field, number))] = value
        else:
            outs[field][number, planes - 1 + VELOCITIES[number][0]] = value

    def put_bottom(field, number, value):
        if VELOCITIES[number][0] == -1:
            down_send[DOWN.index((field, number))] = value
        else:
            outs[field][number, VELOCITIES[number][0]] = value

    for copy in slides:
        copy.wait()
    start_lo, start_hi = rows - residue, residue
    phi_ref[0] = phi_lo[pl.ds(start_lo, rows), :]
    phi_ref[planes + 1] = phi_hi[pl.ds(start_hi, rows), :]

    part_one, part_two = pl.ds(0, FIRST), pl.ds(FIRST, len(UP) - FIRST)

    def send_up(part, recv):
        return [
            send(up_send.at[part], recv.at[:, high], next_near),
            send(up_send.at[part], recv.at[:, low], next_far),
        ]

    def send_down(part, recv):
        return [
            send(down_send.at[part], recv.at[:, low], prev_near),
            send(down_send.at[part], recv.at[:, high], prev_far),
        ]

    collide(planes - 1, put_top)
    first_up = send_up(part_one, lo_one)
    z_top = send(z_send.at[planes - 1], z_recv.at[planes - 1], z_other)
    collide(0, put_bottom)
    first_down = send_down(part_one, hi_one)
    z_bottom = send(z_send.at[0], z_recv.at[0], z_other)

    def along_z(x, k, field, number, value):
        plane = z_recv[x, field * 5 + k]
        if VELOCITIES[number][2] == 1:
            return pltpu.roll(jnp.where(lane_last, plane, value), 1, 1)
        return pltpu.roll(jnp.where(lane_first, plane, value), lanes - 1, 1)

    z_top.wait_recv()
    for field in range(2):
        for number in (4, 5):
            slot = UP.index((field, number))
            up_send[slot] = along_z(planes - 1, 0, field, number, up_send[slot])
    second_up = send_up(part_two, lo_two)
    z_bottom.wait_recv()
    for field in range(2):
        for number in (9, 10):
            slot = DOWN.index((field, number))
            down_send[slot] = along_z(0, 1, field, number, down_send[slot])
    second_down = send_down(part_two, hi_two)
    z_mid.wait_recv()

    for field in range(2):
        for k, pair in enumerate(Z_PAIRS):
            for number in pair:
                step = VELOCITIES[number][0]
                for x in range(max(0, -step), planes - max(0, step)):
                    outs[field][number, x + step] = along_z(
                        x, k, field, number, outs[field][number, x + step]
                    )

    def stays(number):
        step = VELOCITIES[number][0]
        return range(max(0, step), planes + min(0, step))

    for field in range(2):
        for k in range(5):
            for side, numbers, edge in ((0, Y_UP, rows - 1), (1, Y_DOWN, 0)):
                for x in stays(numbers[k]):
                    spot = (field * 5 + k) * planes + x
                    y_send[side, spot : spot + 1, :] = outs[field][
                        numbers[k], x, edge : edge + 1, :
                    ]
    y_up = send(y_send.at[0], y_recv.at[0], y_next)
    y_down = send(y_send.at[1], y_recv.at[1], y_prev)
    y_up.wait_recv()
    y_down.wait_recv()
    for field in range(2):
        for k in range(5):
            for x in stays(Y_UP[k]):
                spot = (field * 5 + k) * planes + x
                index = Y_UP[k]
                outs[field][index, x] = jnp.where(
                    row_first, y_recv[0, spot : spot + 1, :], pltpu.roll(outs[field][index, x], 1, 0)
                )
            for x in stays(Y_DOWN[k]):
                spot = (field * 5 + k) * planes + x
                index = Y_DOWN[k]
                outs[field][index, x] = jnp.where(
                    row_last,
                    y_recv[1, spot : spot + 1, :],
                    pltpu.roll(outs[field][index, x], rows - 1, 0),
                )

    def land(offset, lo_recv, hi_recv):
        for slot in range(lo_recv.shape[0]):
            field, number = UP[offset + slot]
            begin = start_lo - VELOCITIES[number][1]
            outs[field][number, 0] = lo_recv[slot, pl.ds(begin, rows), :]
            field, number = DOWN[offset + slot]
            begin = start_hi - VELOCITIES[number][1]
            outs[field][number, planes - 1] = hi_recv[slot, pl.ds(begin, rows), :]

    for copy in first_up + first_down:
        copy.wait()
    land(0, lo_one, hi_one)
    for copy in second_up + second_down:
        copy.wait()
    land(FIRST, lo_two, hi_two)
    for copy in (to_z, to_up, to_down, z_mid, z_top, z_bottom, y_up, y_down):
        copy.wait_send()


def finish(f_in, g_in, f_out, g_out, sem):
    half = f_in.shape[0] // 2 + 1
    copies = []
    for k, (src, dst) in enumerate(((f_in, f_out), (g_in, g_out))):
        for h, span in enumerate((pl.ds(0, half), pl.ds(half, src.shape[0] - half))):
            copy = pltpu.make_async_copy(src.at[span], dst.at[span], sem.at[2 * k + h])
            copy.start()
            copies.append(copy)
    for copy in copies:
        copy.wait()


def local(sizes, f_pop, g_pop, displacement):
    planes, rows, lanes = f_pop.shape[1:]
    block = (rows, lanes)
    f32 = jnp.float32
    crossing = len(UP)
    copies = 20
    f_post, g_post = pl.pallas_call(
        functools.partial(kernel, sizes),
        out_shape=(
            jax.ShapeDtypeStruct(f_pop.shape, f32),
            jax.ShapeDtypeStruct(g_pop.shape, f32),
        ),
        in_specs=[
            pl.BlockSpec(memory_space=pltpu.SMEM),
            pl.BlockSpec(memory_space=pl.ANY),
            pl.BlockSpec(memory_space=pl.ANY),
        ],
        out_specs=[pl.BlockSpec(memory_space=pltpu.VMEM)] * 2,
        scratch_shapes=[
            pltpu.VMEM(f_pop.shape, f32),
            pltpu.VMEM(g_pop.shape, f32),
            pltpu.VMEM((planes + 2,) + block, f32),
            pltpu.VMEM((planes,) + block, f32),
            pltpu.VMEM((2, planes, lanes), f32),
            pltpu.VMEM((2, planes, lanes), f32),
            pltpu.VMEM((2 * rows, lanes), f32),
            pltpu.VMEM((2 * rows, lanes), f32),
            pltpu.VMEM((planes, 10) + block, f32),
            pltpu.VMEM((planes, 10) + block, f32),
            pltpu.VMEM((crossing,) + block, f32),
            pltpu.VMEM((crossing,) + block, f32),
            pltpu.VMEM((FIRST, 2 * rows, lanes), f32),
            pltpu.VMEM((crossing - FIRST, 2 * rows, lanes), f32),
            pltpu.VMEM((FIRST, 2 * rows, lanes), f32),
            pltpu.VMEM((crossing - FIRST, 2 * rows, lanes), f32),
            pltpu.VMEM((2, 10 * planes, lanes), f32),
            pltpu.VMEM((2, 10 * planes, lanes), f32),
            pltpu.SemaphoreType.DMA((2,)),
            pltpu.SemaphoreType.DMA((copies,)),
            pltpu.SemaphoreType.DMA((copies,)),
        ],
        compiler_params=pltpu.CompilerParams(
            collective_id=0, has_side_effects=True, vmem_limit_bytes=53760 * 1024
        ),
    )(displacement, f_pop, g_pop)
    return pl.pallas_call(
        finish,
        out_shape=(
            jax.ShapeDtypeStruct(f_pop.shape, f32),
            jax.ShapeDtypeStruct(g_pop.shape, f32),
        ),
        in_specs=[pl.BlockSpec(memory_space=pl.ANY)] * 2,
        out_specs=[pl.BlockSpec(memory_space=pl.ANY)] * 2,
        scratch_shapes=[pltpu.SemaphoreType.DMA((4,))],
        compiler_params=pltpu.CompilerParams(vmem_limit_bytes=53760 * 1024),
    )(f_post, g_post)


def solution(mesh):
    sizes = tuple(mesh.shape[axis] for axis in ("gx", "gy", "gz"))
    return jax.shard_map(
        functools.partial(local, sizes),
        mesh=mesh,
        in_specs=(P(None, "gx", "gy", "gz"), P(None, "gx", "gy", "gz"), P()),
        out_specs=(P(None, "gx", "gy", "gz"), P(None, "gx", "gy", "gz")),
        check_vma=False,
    )
```

```python
import functools

import jax
import jax.numpy as jnp
from jax import lax
from jax.experimental import pallas as pl
from jax.experimental.pallas import tpu as pltpu
from jax.sharding import PartitionSpec as P

VELOCITIES = [
    (0, 0, 0),
    (1, 0, 0),
    (1, 1, 0),
    (1, -1, 0),
    (1, 0, 1),
    (1, 0, -1),
    (-1, 0, 0),
    (-1, -1, 0),
    (-1, 1, 0),
    (-1, 0, -1),
    (-1, 0, 1),
    (0, 1, 0),
    (0, -1, 0),
    (0, 0, 1),
    (0, 0, -1),
    (0, 1, 1),
    (0, -1, -1),
    (0, 1, -1),
    (0, -1, 1),
]
POPS = 19
TAU_FLUID = 0.8
TAU_ORDER = 0.9
PAIRS = [(1, 6), (2, 7), (3, 8), (4, 9), (5, 10), (11, 12), (13, 14), (15, 16), (17, 18)]
Z_PAIRS = [(4, 5), (10, 9), (13, 14), (15, 16), (18, 17)]
Y_UP = [2, 8, 11, 15, 17]
Y_DOWN = [3, 7, 12, 16, 18]
UP = [(0, 1), (0, 2), (0, 3), (1, 1), (1, 2), (1, 3), (0, 4), (0, 5), (1, 4), (1, 5)]
DOWN = [(0, 6), (0, 7), (0, 8), (1, 6), (1, 7), (1, 8), (0, 9), (0, 10), (1, 9), (1, 10)]
FIRST = 6
MESH = pl.DeviceIdType.MESH


def kernel(
    sizes,
    shift_ref,
    f_hbm,
    g_hbm,
    f_out,
    g_out,
    f_ref,
    g_ref,
    phi_ref,
    phi_z,
    phi_ys,
    phi_yr,
    phi_lo,
    phi_hi,
    z_send,
    z_recv,
    up_send,
    down_send,
    lo_one,
    lo_two,
    hi_one,
    hi_two,
    y_send,
    y_recv,
    local_sem,
    send_sem,
    recv_sem,
):
    count_x, count_y, count_z = sizes
    planes, rows, lanes = f_ref.shape[1:]
    a, b, c = lax.axis_index("gx"), lax.axis_index("gy"), lax.axis_index("gz")
    half = count_y // 2
    outs = (f_out, g_out)

    def at(dx, dy, dz=0):
        return (
            lax.rem(a + dx + count_x, count_x),
            lax.rem(b + dy + count_y, count_y),
            lax.rem(c + dz, count_z),
        )

    next_near, next_far = at(1, half), at(1, half + 1)
    prev_near, prev_far = at(-1, -half), at(-1, -half - 1)
    y_next, y_prev, z_other = at(0, 1), at(0, -1), at(0, 0, 1)

    barrier = pltpu.get_barrier_semaphore()
    partners = (next_near, next_far, prev_near, prev_far, y_next, y_prev, z_other)
    for partner in partners:
        pl.semaphore_signal(barrier, inc=1, device_id=partner, device_id_type=MESH)

    def load(src, dst, parts, base):
        size = -(-POPS // parts)
        copies = []
        for k in range(parts):
            span = pl.ds(k * size, min(size, POPS - k * size))
            copies.append(
                pltpu.make_async_copy(src.at[span], dst.at[span], local_sem.at[base + k])
            )
            copies[-1].start()
        return copies

    load_g = load(g_hbm, g_ref, 4, 0)
    load_f = load(f_hbm, f_ref, 2, 4)

    used = [0]

    def send(src, dst, target):
        slot = used[0]
        used[0] += 1
        copy = pltpu.make_async_remote_copy(
            src_ref=src,
            dst_ref=dst,
            send_sem=send_sem.at[slot],
            recv_sem=recv_sem.at[slot],
            device_id=target,
            device_id_type=MESH,
        )
        copy.start()
        return copy

    for copy in load_g:
        copy.wait()
    for x in range(planes):
        parts = [g_ref[i, x] for i in range(POPS)]
        while len(parts) > 1:
            parts = [
                parts[k] + parts[k + 1] if k + 1 < len(parts) else parts[k]
                for k in range(0, len(parts), 2)
            ]
        phi_ref[x + 1] = parts[0]
        phi_ys[0, x : x + 1, :] = parts[0][rows - 1 : rows]
        phi_ys[1, x : x + 1, :] = parts[0][0:1]
    pl.semaphore_wait(barrier, len(partners))

    low, high = pl.ds(0, rows), pl.ds(rows, rows)
    last = planes
    slides = [
        send(phi_ref.at[last], phi_lo.at[low], next_far),
        send(phi_ref.at[last], phi_lo.at[high], next_near),
        send(phi_ref.at[1], phi_hi.at[low], prev_near),
        send(phi_ref.at[1], phi_hi.at[high], prev_far),
    ]
    to_z = send(phi_ref.at[pl.ds(1, planes)], phi_z, z_other)
    to_up = send(phi_ys.at[0], phi_yr.at[0], y_next)
    to_down = send(phi_ys.at[1], phi_yr.at[1], y_prev)

    lane = lax.broadcasted_iota(jnp.int32, (rows, lanes), 1)
    row = lax.broadcasted_iota(jnp.int32, (rows, lanes), 0)
    lane_first, lane_last = lane == 0, lane == lanes - 1
    row_first, row_last = row == 0, row == rows - 1
    residue = jnp.clip(shift_ref[0] - half * rows, 1, rows - 1)

    def collide(x, put):
        phi = phi_ref[x + 1]
        xm, xp = phi_ref[x], phi_ref[x + 2]
        ym = jnp.where(row_first, phi_yr[0, pl.ds(x, 1), :], pltpu.roll(phi, 1, 0))
        yp = jnp.where(row_last, phi_yr[1, pl.ds(x, 1), :], pltpu.roll(phi, rows - 1, 0))
        other = phi_z[x]
        zm = pltpu.roll(jnp.where(lane_last, other, phi), 1, 1)
        zp = pltpu.roll(jnp.where(lane_first, other, phi), lanes - 1, 1)
        laplace = xm + xp + ym + yp + zm + zp - 6.0 * phi
        chemical = 0.5 * (phi * phi * phi - phi) - 0.5 * laplace
        half_mu = 0.5 * chemical
        force = [half_mu * (xp - xm), half_mu * (yp - ym), half_mu * (zp - zm)]
        f = [f_ref[i, x] for i in range(POPS)]
        even_sum = f[0]
        moment = [None, None, None]
        for plus, minus in PAIRS:
            even_sum = even_sum + (f[plus] + f[minus])
            diff = f[plus] - f[minus]
            for axis in range(3):
                comp = VELOCITIES[plus][axis]
                if comp:
                    if moment[axis] is None:
                        moment[axis] = diff
                    elif comp > 0:
                        moment[axis] = moment[axis] + diff
                    else:
                        moment[axis] = moment[axis] - diff
        density = even_sum
        inverse = 1.0 / density
        flow = [(moment[axis] + 0.5 * force[axis]) * inverse for axis in range(3)]
        usq = flow[0] * flow[0] + flow[1] * flow[1] + flow[2] * flow[2]
        flow_force = flow[0] * force[0] + flow[1] * force[1] + flow[2] * force[2]

        inv_f, inv_g = 1.0 / TAU_FLUID, 1.0 / TAU_ORDER
        keep_f, keep_g = 1.0 - inv_f, 1.0 - inv_g
        gain = 1.0 - 0.5 / TAU_FLUID
        f_base = inv_f * density * (1.0 - 1.5 * usq) - (3.0 * gain) * flow_force
        f_square = (4.5 * inv_f) * density
        f_line = (3.0 * inv_f) * density
        g_base = inv_g * (3.0 * chemical - 1.5 * phi * usq)
        g_square = (4.5 * inv_g) * phi
        g_line = (3.0 * inv_g) * phi
        put(0, 0, keep_f * f[0] + (1.0 / 3.0) * f_base)
        put(1, 0, keep_g * g_ref[0, x] + inv_g * (phi - 2.0 * chemical - 0.5 * phi * usq))

        def dot(number, values):
            total = None
            for axis in range(3):
                comp = VELOCITIES[number][axis]
                if comp:
                    if total is None:
                        total = values[axis] if comp > 0 else -values[axis]
                    else:
                        total = total + values[axis] if comp > 0 else total - values[axis]
            return total

        done = {}
        for plus, minus in PAIRS:
            weight = 1.0 / 18.0 if sum(abs(v) for v in VELOCITIES[plus]) == 1 else 1.0 / 36.0
            cu = dot(plus, flow)
            cf = dot(plus, force)
            f_even = weight * (f_base + cu * (f_square * cu + (9.0 * gain) * cf))
            f_odd = weight * (f_line * cu + (3.0 * gain) * cf)
            g_even = weight * (g_base + g_square * (cu * cu))
            g_odd = weight * (g_line * cu)
            done[0, plus] = keep_f * f[plus] + (f_even + f_odd)
            done[0, minus] = keep_f * f[minus] + (f_even - f_odd)
            done[1, plus] = keep_g * g_ref[plus, x] + (g_even + g_odd)
            done[1, minus] = keep_g * g_ref[minus, x] + (g_even - g_odd)
        for (field, number), value in done.items():
            put(field, number, value)
        for field in range(2):
            for k, (plus, minus) in enumerate(Z_PAIRS):
                z_send[x, field * 5 + k] = jnp.where(
                    lane_last, done[field, plus], done[field, minus]
                )

    to_z.wait_recv()
    to_up.wait_recv()
    to_down.wait_recv()
    for copy in load_f:
        copy.wait()

    def inner(x, carry):
        def put(field, number, value):
            outs[field][number, x + VELOCITIES[number][0]] = value

        collide(x, put)
        return carry

    lax.fori_loop(1, planes - 1, inner, 0)
    middle = pl.ds(1, planes - 2)
    z_mid = send(z_send.at[middle], z_recv.at[middle], z_other)

    def put_top(field, number, value):
        if VELOCITIES[number][0] == 1:
            up_send[UP.index((field, number))] = value
        else:
            outs[field][number, planes - 1 + VELOCITIES[number][0]] = value

    def put_bottom(field, number, value):
        if VELOCITIES[number][0] == -1:
            down_send[DOWN.index((field, number))] = value
        else:
            outs[field][number, VELOCITIES[number][0]] = value

    for copy in slides:
        copy.wait()
    start_lo, start_hi = rows - residue, residue
    phi_ref[0] = phi_lo[pl.ds(start_lo, rows), :]
    phi_ref[planes + 1] = phi_hi[pl.ds(start_hi, rows), :]

    part_one, part_two = pl.ds(0, FIRST), pl.ds(FIRST, len(UP) - FIRST)

    def send_up(part, recv):
        return [
            send(up_send.at[part], recv.at[:, high], next_near),
            send(up_send.at[part], recv.at[:, low], next_far),
        ]

    def send_down(part, recv):
        return [
            send(down_send.at[part], recv.at[:, low], prev_near),
            send(down_send.at[part], recv.at[:, high], prev_far),
        ]

    collide(planes - 1, put_top)
    z_top = send(z_send.at[planes - 1], z_recv.at[planes - 1], z_other)
    first_up = send_up(part_one, lo_one)
    collide(0, put_bottom)
    z_bottom = send(z_send.at[0], z_recv.at[0], z_other)
    first_down = send_down(part_one, hi_one)

    def along_z(x, k, field, number, value):
        plane = z_recv[x, field * 5 + k]
        if VELOCITIES[number][2] == 1:
            return pltpu.roll(jnp.where(lane_last, plane, value), 1, 1)
        return pltpu.roll(jnp.where(lane_first, plane, value), lanes - 1, 1)

    z_top.wait_recv()
    for field in range(2):
        for number in (4, 5):
            slot = UP.index((field, number))
            up_send[slot] = along_z(planes - 1, 0, field, number, up_send[slot])
    second_up = send_up(part_two, lo_two)
    z_bottom.wait_recv()
    for field in range(2):
        for number in (9, 10):
            slot = DOWN.index((field, number))
            down_send[slot] = along_z(0, 1, field, number, down_send[slot])
    second_down = send_down(part_two, hi_two)
    z_mid.wait_recv()

    for field in range(2):
        for k, pair in enumerate(Z_PAIRS):
            for number in pair:
                step = VELOCITIES[number][0]
                for x in range(max(0, -step), planes - max(0, step)):
                    outs[field][number, x + step] = along_z(
                        x, k, field, number, outs[field][number, x + step]
                    )

    def stays(number):
        step = VELOCITIES[number][0]
        return range(max(0, step), planes + min(0, step))

    for field in range(2):
        for k in range(5):
            for side, numbers, edge in ((0, Y_UP, rows - 1), (1, Y_DOWN, 0)):
                for x in stays(numbers[k]):
                    spot = (field * 5 + k) * planes + x
                    y_send[side, spot : spot + 1, :] = outs[field][
                        numbers[k], x, edge : edge + 1, :
                    ]
    y_up = send(y_send.at[0], y_recv.at[0], y_next)
    y_down = send(y_send.at[1], y_recv.at[1], y_prev)
    y_up.wait_recv()
    y_down.wait_recv()
    for field in range(2):
        for k in range(5):
            for x in stays(Y_UP[k]):
                spot = (field * 5 + k) * planes + x
                index = Y_UP[k]
                outs[field][index, x] = jnp.where(
                    row_first, y_recv[0, spot : spot + 1, :], pltpu.roll(outs[field][index, x], 1, 0)
                )
            for x in stays(Y_DOWN[k]):
                spot = (field * 5 + k) * planes + x
                index = Y_DOWN[k]
                outs[field][index, x] = jnp.where(
                    row_last,
                    y_recv[1, spot : spot + 1, :],
                    pltpu.roll(outs[field][index, x], rows - 1, 0),
                )

    def land(offset, lo_recv, hi_recv):
        for slot in range(lo_recv.shape[0]):
            field, number = UP[offset + slot]
            begin = start_lo - VELOCITIES[number][1]
            outs[field][number, 0] = lo_recv[slot, pl.ds(begin, rows), :]
            field, number = DOWN[offset + slot]
            begin = start_hi - VELOCITIES[number][1]
            outs[field][number, planes - 1] = hi_recv[slot, pl.ds(begin, rows), :]

    for copy in first_up + first_down:
        copy.wait()
    land(0, lo_one, hi_one)
    for copy in second_up + second_down:
        copy.wait()
    land(FIRST, lo_two, hi_two)
    for copy in (to_z, to_up, to_down, z_mid, z_top, z_bottom, y_up, y_down):
        copy.wait_send()


def finish(f_in, g_in, f_out, g_out, sem):
    half = f_in.shape[0] // 2 + 1
    copies = []
    for k, (src, dst) in enumerate(((f_in, f_out), (g_in, g_out))):
        for h, span in enumerate((pl.ds(0, half), pl.ds(half, src.shape[0] - half))):
            copy = pltpu.make_async_copy(src.at[span], dst.at[span], sem.at[2 * k + h])
            copy.start()
            copies.append(copy)
    for copy in copies:
        copy.wait()


def local(sizes, f_pop, g_pop, displacement):
    planes, rows, lanes = f_pop.shape[1:]
    block = (rows, lanes)
    f32 = jnp.float32
    crossing = len(UP)
    copies = 20
    f_post, g_post = pl.pallas_call(
        functools.partial(kernel, sizes),
        out_shape=(
            jax.ShapeDtypeStruct(f_pop.shape, f32),
            jax.ShapeDtypeStruct(g_pop.shape, f32),
        ),
        in_specs=[
            pl.BlockSpec(memory_space=pltpu.SMEM),
            pl.BlockSpec(memory_space=pl.ANY),
            pl.BlockSpec(memory_space=pl.ANY),
        ],
        out_specs=[pl.BlockSpec(memory_space=pltpu.VMEM)] * 2,
        scratch_shapes=[
            pltpu.VMEM(f_pop.shape, f32),
            pltpu.VMEM(g_pop.shape, f32),
            pltpu.VMEM((planes + 2,) + block, f32),
            pltpu.VMEM((planes,) + block, f32),
            pltpu.VMEM((2, planes, lanes), f32),
            pltpu.VMEM((2, planes, lanes), f32),
            pltpu.VMEM((2 * rows, lanes), f32),
            pltpu.VMEM((2 * rows, lanes), f32),
            pltpu.VMEM((planes, 10) + block, f32),
            pltpu.VMEM((planes, 10) + block, f32),
            pltpu.VMEM((crossing,) + block, f32),
            pltpu.VMEM((crossing,) + block, f32),
            pltpu.VMEM((FIRST, 2 * rows, lanes), f32),
            pltpu.VMEM((crossing - FIRST, 2 * rows, lanes), f32),
            pltpu.VMEM((FIRST, 2 * rows, lanes), f32),
            pltpu.VMEM((crossing - FIRST, 2 * rows, lanes), f32),
            pltpu.VMEM((2, 10 * planes, lanes), f32),
            pltpu.VMEM((2, 10 * planes, lanes), f32),
            pltpu.SemaphoreType.DMA((6,)),
            pltpu.SemaphoreType.DMA((copies,)),
            pltpu.SemaphoreType.DMA((copies,)),
        ],
        compiler_params=pltpu.CompilerParams(
            collective_id=0, has_side_effects=True, vmem_limit_bytes=53760 * 1024
        ),
    )(displacement, f_pop, g_pop)
    return pl.pallas_call(
        finish,
        out_shape=(
            jax.ShapeDtypeStruct(f_pop.shape, f32),
            jax.ShapeDtypeStruct(g_pop.shape, f32),
        ),
        in_specs=[pl.BlockSpec(memory_space=pl.ANY)] * 2,
        out_specs=[pl.BlockSpec(memory_space=pl.ANY)] * 2,
        scratch_shapes=[pltpu.SemaphoreType.DMA((4,))],
        compiler_params=pltpu.CompilerParams(vmem_limit_bytes=53760 * 1024),
    )(f_post, g_post)


def solution(mesh):
    sizes = tuple(mesh.shape[axis] for axis in ("gx", "gy", "gz"))
    return jax.shard_map(
        functools.partial(local, sizes),
        mesh=mesh,
        in_specs=(P(None, "gx", "gy", "gz"), P(None, "gx", "gy", "gz"), P()),
        out_specs=(P(None, "gx", "gy", "gz"), P(None, "gx", "gy", "gz")),
        check_vma=False,
    )
```

```python
import functools

import jax
import jax.numpy as jnp
from jax import lax
from jax.experimental import pallas as pl
from jax.experimental.pallas import tpu as pltpu
from jax.sharding import PartitionSpec as P

VELOCITIES = [
    (0, 0, 0),
    (1, 0, 0),
    (1, 1, 0),
    (1, -1, 0),
    (1, 0, 1),
    (1, 0, -1),
    (-1, 0, 0),
    (-1, -1, 0),
    (-1, 1, 0),
    (-1, 0, -1),
    (-1, 0, 1),
    (0, 1, 0),
    (0, -1, 0),
    (0, 0, 1),
    (0, 0, -1),
    (0, 1, 1),
    (0, -1, -1),
    (0, 1, -1),
    (0, -1, 1),
]
POPS = 19
TAU_FLUID = 0.8
TAU_ORDER = 0.9
PAIRS = [(1, 6), (2, 7), (3, 8), (4, 9), (5, 10), (11, 12), (13, 14), (15, 16), (17, 18)]
Z_PAIRS = [(4, 5), (10, 9), (13, 14), (15, 16), (18, 17)]
Y_UP = [2, 8, 11, 15, 17]
Y_DOWN = [3, 7, 12, 16, 18]
UP = [(0, 1), (0, 2), (0, 3), (1, 1), (1, 2), (1, 3), (0, 4), (0, 5), (1, 4), (1, 5)]
DOWN = [(0, 6), (0, 7), (0, 8), (1, 6), (1, 7), (1, 8), (0, 9), (0, 10), (1, 9), (1, 10)]
FIRST = 6
MESH = pl.DeviceIdType.MESH


def kernel(
    sizes,
    shift_ref,
    f_hbm,
    g_hbm,
    f_out,
    g_out,
    f_ref,
    g_ref,
    phi_ref,
    phi_z,
    phi_ys,
    phi_yr,
    phi_lo,
    phi_hi,
    z_send,
    z_recv,
    up_send,
    down_send,
    lo_one,
    lo_two,
    hi_one,
    hi_two,
    y_send,
    y_recv,
    local_sem,
    send_sem,
    recv_sem,
):
    count_x, count_y, count_z = sizes
    planes, rows, lanes = f_ref.shape[1:]
    a, b, c = lax.axis_index("gx"), lax.axis_index("gy"), lax.axis_index("gz")
    half = count_y // 2
    outs = (f_out, g_out)

    def at(dx, dy, dz=0):
        return (
            lax.rem(a + dx + count_x, count_x),
            lax.rem(b + dy + count_y, count_y),
            lax.rem(c + dz, count_z),
        )

    next_near, next_far = at(1, half), at(1, half + 1)
    prev_near, prev_far = at(-1, -half), at(-1, -half - 1)
    y_next, y_prev, z_other = at(0, 1), at(0, -1), at(0, 0, 1)

    load_g = pltpu.make_async_copy(g_hbm, g_ref, local_sem.at[0])
    load_f = pltpu.make_async_copy(f_hbm, f_ref, local_sem.at[1])
    load_g.start()
    load_f.start()
    barrier = pltpu.get_barrier_semaphore()
    partners = (next_near, next_far, prev_near, prev_far, y_next, y_prev, z_other)
    for partner in partners:
        pl.semaphore_signal(barrier, inc=1, device_id=partner, device_id_type=MESH)

    used = [0]

    def send(src, dst, target):
        slot = used[0]
        used[0] += 1
        copy = pltpu.make_async_remote_copy(
            src_ref=src,
            dst_ref=dst,
            send_sem=send_sem.at[slot],
            recv_sem=recv_sem.at[slot],
            device_id=target,
            device_id_type=MESH,
        )
        copy.start()
        return copy

    load_g.wait()
    for x in range(planes):
        parts = [g_ref[i, x] for i in range(POPS)]
        while len(parts) > 1:
            parts = [
                parts[k] + parts[k + 1] if k + 1 < len(parts) else parts[k]
                for k in range(0, len(parts), 2)
            ]
        phi_ref[x + 1] = parts[0]
        phi_ys[0, x : x + 1, :] = parts[0][rows - 1 : rows]
        phi_ys[1, x : x + 1, :] = parts[0][0:1]
    pl.semaphore_wait(barrier, len(partners))

    low, high = pl.ds(0, rows), pl.ds(rows, rows)
    last = planes
    slides = [
        send(phi_ref.at[last], phi_lo.at[low], next_far),
        send(phi_ref.at[last], phi_lo.at[high], next_near),
        send(phi_ref.at[1], phi_hi.at[low], prev_near),
        send(phi_ref.at[1], phi_hi.at[high], prev_far),
    ]
    to_z = send(phi_ref.at[pl.ds(1, planes)], phi_z, z_other)
    to_up = send(phi_ys.at[0], phi_yr.at[0], y_next)
    to_down = send(phi_ys.at[1], phi_yr.at[1], y_prev)

    lane = lax.broadcasted_iota(jnp.int32, (rows, lanes), 1)
    row = lax.broadcasted_iota(jnp.int32, (rows, lanes), 0)
    lane_first, lane_last = lane == 0, lane == lanes - 1
    row_first, row_last = row == 0, row == rows - 1
    residue = jnp.clip(shift_ref[0] - half * rows, 1, rows - 1)

    def collide(x, put):
        phi = phi_ref[x + 1]
        xm, xp = phi_ref[x], phi_ref[x + 2]
        ym = jnp.where(row_first, phi_yr[0, pl.ds(x, 1), :], pltpu.roll(phi, 1, 0))
        yp = jnp.where(row_last, phi_yr[1, pl.ds(x, 1), :], pltpu.roll(phi, rows - 1, 0))
        other = phi_z[x]
        zm = pltpu.roll(jnp.where(lane_last, other, phi), 1, 1)
        zp = pltpu.roll(jnp.where(lane_first, other, phi), lanes - 1, 1)
        laplace = xm + xp + ym + yp + zm + zp - 6.0 * phi
        chemical = 0.5 * (phi * phi * phi - phi) - 0.5 * laplace
        half_mu = 0.5 * chemical
        force = [half_mu * (xp - xm), half_mu * (yp - ym), half_mu * (zp - zm)]
        f = [f_ref[i, x] for i in range(POPS)]
        even_sum = f[0]
        moment = [None, None, None]
        for plus, minus in PAIRS:
            even_sum = even_sum + (f[plus] + f[minus])
            diff = f[plus] - f[minus]
            for axis in range(3):
                comp = VELOCITIES[plus][axis]
                if comp:
                    if moment[axis] is None:
                        moment[axis] = diff
                    elif comp > 0:
                        moment[axis] = moment[axis] + diff
                    else:
                        moment[axis] = moment[axis] - diff
        density = even_sum
        inverse = 1.0 / density
        flow = [(moment[axis] + 0.5 * force[axis]) * inverse for axis in range(3)]
        usq = flow[0] * flow[0] + flow[1] * flow[1] + flow[2] * flow[2]
        flow_force = flow[0] * force[0] + flow[1] * force[1] + flow[2] * force[2]

        inv_f, inv_g = 1.0 / TAU_FLUID, 1.0 / TAU_ORDER
        keep_f, keep_g = 1.0 - inv_f, 1.0 - inv_g
        gain = 1.0 - 0.5 / TAU_FLUID
        f_base = inv_f * density * (1.0 - 1.5 * usq) - (3.0 * gain) * flow_force
        f_square = (4.5 * inv_f) * density
        f_line = (3.0 * inv_f) * density
        g_base = inv_g * (3.0 * chemical - 1.5 * phi * usq)
        g_square = (4.5 * inv_g) * phi
        g_line = (3.0 * inv_g) * phi
        put(0, 0, keep_f * f[0] + (1.0 / 3.0) * f_base)
        put(1, 0, keep_g * g_ref[0, x] + inv_g * (phi - 2.0 * chemical - 0.5 * phi * usq))

        def dot(number, values):
            total = None
            for axis in range(3):
                comp = VELOCITIES[number][axis]
                if comp:
                    if total is None:
                        total = values[axis] if comp > 0 else -values[axis]
                    else:
                        total = total + values[axis] if comp > 0 else total - values[axis]
            return total

        done = {}
        for plus, minus in PAIRS:
            weight = 1.0 / 18.0 if sum(abs(v) for v in VELOCITIES[plus]) == 1 else 1.0 / 36.0
            cu = dot(plus, flow)
            cf = dot(plus, force)
            f_even = weight * (f_base + cu * (f_square * cu + (9.0 * gain) * cf))
            f_odd = weight * (f_line * cu + (3.0 * gain) * cf)
            g_even = weight * (g_base + g_square * (cu * cu))
            g_odd = weight * (g_line * cu)
            done[0, plus] = keep_f * f[plus] + (f_even + f_odd)
            done[0, minus] = keep_f * f[minus] + (f_even - f_odd)
            done[1, plus] = keep_g * g_ref[plus, x] + (g_even + g_odd)
            done[1, minus] = keep_g * g_ref[minus, x] + (g_even - g_odd)
        for (field, number), value in done.items():
            put(field, number, value)
        for field in range(2):
            for k, (plus, minus) in enumerate(Z_PAIRS):
                z_send[x, field * 5 + k] = jnp.where(
                    lane_last, done[field, plus], done[field, minus]
                )

    to_z.wait_recv()
    to_up.wait_recv()
    to_down.wait_recv()
    load_f.wait()

    def inner(x, carry):
        def put(field, number, value):
            outs[field][number, x + VELOCITIES[number][0]] = value

        collide(x, put)
        return carry

    lax.fori_loop(1, planes - 1, inner, 0)
    middle = pl.ds(1, planes - 2)
    z_mid = send(z_send.at[middle], z_recv.at[middle], z_other)

    def put_top(field, number, value):
        if VELOCITIES[number][0] == 1:
            up_send[UP.index((field, number))] = value
        else:
            outs[field][number, planes - 1 + VELOCITIES[number][0]] = value

    def put_bottom(field, number, value):
        if VELOCITIES[number][0] == -1:
            down_send[DOWN.index((field, number))] = value
        else:
            outs[field][number, VELOCITIES[number][0]] = value

    for copy in slides:
        copy.wait()
    start_lo, start_hi = rows - residue, residue
    phi_ref[0] = phi_lo[pl.ds(start_lo, rows), :]
    phi_ref[planes + 1] = phi_hi[pl.ds(start_hi, rows), :]

    part_one, part_two = pl.ds(0, FIRST), pl.ds(FIRST, len(UP) - FIRST)

    def send_up(part, recv):
        return [
            send(up_send.at[part], recv.at[:, high], next_near),
            send(up_send.at[part], recv.at[:, low], next_far),
        ]

    def send_down(part, recv):
        return [
            send(down_send.at[part], recv.at[:, low], prev_near),
            send(down_send.at[part], recv.at[:, high], prev_far),
        ]

    collide(planes - 1, put_top)
    z_top = send(z_send.at[planes - 1], z_recv.at[planes - 1], z_other)
    collide(0, put_bottom)
    first = [
        send(up_send.at[part_one], lo_one.at[:, high], next_near),
        send(down_send.at[part_one], hi_one.at[:, low], prev_near),
        send(up_send.at[part_one], lo_one.at[:, low], next_far),
        send(down_send.at[part_one], hi_one.at[:, high], prev_far),
    ]
    z_bottom = send(z_send.at[0], z_recv.at[0], z_other)

    def along_z(x, k, field, number, value):
        plane = z_recv[x, field * 5 + k]
        if VELOCITIES[number][2] == 1:
            return pltpu.roll(jnp.where(lane_last, plane, value), 1, 1)
        return pltpu.roll(jnp.where(lane_first, plane, value), lanes - 1, 1)

    z_top.wait_recv()
    for field in range(2):
        for number in (4, 5):
            slot = UP.index((field, number))
            up_send[slot] = along_z(planes - 1, 0, field, number, up_send[slot])
    second_up = send_up(part_two, lo_two)
    z_bottom.wait_recv()
    for field in range(2):
        for number in (9, 10):
            slot = DOWN.index((field, number))
            down_send[slot] = along_z(0, 1, field, number, down_send[slot])
    second_down = send_down(part_two, hi_two)
    z_mid.wait_recv()

    for field in range(2):
        for k, pair in enumerate(Z_PAIRS):
            for number in pair:
                step = VELOCITIES[number][0]
                for x in range(max(0, -step), planes - max(0, step)):
                    outs[field][number, x + step] = along_z(
                        x, k, field, number, outs[field][number, x + step]
                    )

    def stays(number):
        step = VELOCITIES[number][0]
        return range(max(0, step), planes + min(0, step))

    for field in range(2):
        for k in range(5):
            for side, numbers, edge in ((0, Y_UP, rows - 1), (1, Y_DOWN, 0)):
                for x in stays(numbers[k]):
                    spot = (field * 5 + k) * planes + x
                    y_send[side, spot : spot + 1, :] = outs[field][
                        numbers[k], x, edge : edge + 1, :
                    ]
    y_up = send(y_send.at[0], y_recv.at[0], y_next)
    y_down = send(y_send.at[1], y_recv.at[1], y_prev)
    y_up.wait_recv()
    y_down.wait_recv()
    for field in range(2):
        for k in range(5):
            for x in stays(Y_UP[k]):
                spot = (field * 5 + k) * planes + x
                index = Y_UP[k]
                outs[field][index, x] = jnp.where(
                    row_first, y_recv[0, spot : spot + 1, :], pltpu.roll(outs[field][index, x], 1, 0)
                )
            for x in stays(Y_DOWN[k]):
                spot = (field * 5 + k) * planes + x
                index = Y_DOWN[k]
                outs[field][index, x] = jnp.where(
                    row_last,
                    y_recv[1, spot : spot + 1, :],
                    pltpu.roll(outs[field][index, x], rows - 1, 0),
                )

    def land(offset, lo_recv, hi_recv):
        for slot in range(lo_recv.shape[0]):
            field, number = UP[offset + slot]
            begin = start_lo - VELOCITIES[number][1]
            outs[field][number, 0] = lo_recv[slot, pl.ds(begin, rows), :]
            field, number = DOWN[offset + slot]
            begin = start_hi - VELOCITIES[number][1]
            outs[field][number, planes - 1] = hi_recv[slot, pl.ds(begin, rows), :]

    for copy in first:
        copy.wait()
    land(0, lo_one, hi_one)
    for copy in second_up + second_down:
        copy.wait()
    land(FIRST, lo_two, hi_two)
    for copy in (to_z, to_up, to_down, z_mid, z_top, z_bottom, y_up, y_down):
        copy.wait_send()


def finish(f_in, g_in, f_out, g_out, sem):
    half = f_in.shape[0] // 2 + 1
    copies = []
    for k, (src, dst) in enumerate(((f_in, f_out), (g_in, g_out))):
        for h, span in enumerate((pl.ds(0, half), pl.ds(half, src.shape[0] - half))):
            copy = pltpu.make_async_copy(src.at[span], dst.at[span], sem.at[2 * k + h])
            copy.start()
            copies.append(copy)
    for copy in copies:
        copy.wait()


def local(sizes, f_pop, g_pop, displacement):
    planes, rows, lanes = f_pop.shape[1:]
    block = (rows, lanes)
    f32 = jnp.float32
    crossing = len(UP)
    copies = 20
    f_post, g_post = pl.pallas_call(
        functools.partial(kernel, sizes),
        out_shape=(
            jax.ShapeDtypeStruct(f_pop.shape, f32),
            jax.ShapeDtypeStruct(g_pop.shape, f32),
        ),
        in_specs=[
            pl.BlockSpec(memory_space=pltpu.SMEM),
            pl.BlockSpec(memory_space=pl.ANY),
            pl.BlockSpec(memory_space=pl.ANY),
        ],
        out_specs=[pl.BlockSpec(memory_space=pltpu.VMEM)] * 2,
        scratch_shapes=[
            pltpu.VMEM(f_pop.shape, f32),
            pltpu.VMEM(g_pop.shape, f32),
            pltpu.VMEM((planes + 2,) + block, f32),
            pltpu.VMEM((planes,) + block, f32),
            pltpu.VMEM((2, planes, lanes), f32),
            pltpu.VMEM((2, planes, lanes), f32),
            pltpu.VMEM((2 * rows, lanes), f32),
            pltpu.VMEM((2 * rows, lanes), f32),
            pltpu.VMEM((planes, 10) + block, f32),
            pltpu.VMEM((planes, 10) + block, f32),
            pltpu.VMEM((crossing,) + block, f32),
            pltpu.VMEM((crossing,) + block, f32),
            pltpu.VMEM((FIRST, 2 * rows, lanes), f32),
            pltpu.VMEM((crossing - FIRST, 2 * rows, lanes), f32),
            pltpu.VMEM((FIRST, 2 * rows, lanes), f32),
            pltpu.VMEM((crossing - FIRST, 2 * rows, lanes), f32),
            pltpu.VMEM((2, 10 * planes, lanes), f32),
            pltpu.VMEM((2, 10 * planes, lanes), f32),
            pltpu.SemaphoreType.DMA((2,)),
            pltpu.SemaphoreType.DMA((copies,)),
            pltpu.SemaphoreType.DMA((copies,)),
        ],
        compiler_params=pltpu.CompilerParams(
            collective_id=0, has_side_effects=True, vmem_limit_bytes=53760 * 1024
        ),
    )(displacement, f_pop, g_pop)
    return pl.pallas_call(
        finish,
        out_shape=(
            jax.ShapeDtypeStruct(f_pop.shape, f32),
            jax.ShapeDtypeStruct(g_pop.shape, f32),
        ),
        in_specs=[pl.BlockSpec(memory_space=pl.ANY)] * 2,
        out_specs=[pl.BlockSpec(memory_space=pl.ANY)] * 2,
        scratch_shapes=[pltpu.SemaphoreType.DMA((4,))],
        compiler_params=pltpu.CompilerParams(vmem_limit_bytes=53760 * 1024),
    )(f_post, g_post)


def solution(mesh):
    sizes = tuple(mesh.shape[axis] for axis in ("gx", "gy", "gz"))
    return jax.shard_map(
        functools.partial(local, sizes),
        mesh=mesh,
        in_specs=(P(None, "gx", "gy", "gz"), P(None, "gx", "gy", "gz"), P()),
        out_specs=(P(None, "gx", "gy", "gz"), P(None, "gx", "gy", "gz")),
        check_vma=False,
    )
```
